32 devices in a mesh: section: 2 (over core), row: 4 (over z), col: 4 (over y, x).
Axes of the slice: x: 2, y: 2, z: 4, core: 2. Of those that a mesh axis runs over, the one named last changes fastest.
Arguments:
- inputs: bfloat16 [2, 512, 6144], P(None, 'row'), may hold values from -6 to 6
- norm_gain: float32 [2, 6144], P('section'), may hold values from 0.1 to 1.9
- w_in: bfloat16 [2, 4, 4, 64, 128, 128], P('section', 'row', 'col'), may hold values from -0.3125 to 0.3125
- w_in_slot: int32 [2, 4, 4, 64], P('section', 'row', 'col'), may hold values from 0 to 575, as said below
- w_in_count: int32 [2, 4, 4], P('section', 'row', 'col'), may hold values from 16 to 64, as said below
- w_out: bfloat16 [2, 4, 4, 64, 128, 128], P('section', 'row', 'col'), may hold values from -0.15625 to 0.15625
- w_out_slot: int32 [2, 4, 4, 64], P('section', 'row', 'col'), may hold values from 0 to 575, as said below
- w_out_count: int32 [2, 4, 4], P('section', 'row', 'col'), may hold values from 16 to 64, as said below
Outputs:
- phase_outputs: bfloat16 [2, 2, 512, 6144], P('section', None, 'row', 'col')
The draws below stay inside these ranges and needn't reach their ends.
Inputs may be any that keep to these rules, and one draw needn't show every extreme that they name: `w_in_slot`: positions p = d * 48 + f of a block in its cell's 12 x 48 grid of blocks; distinct within a cell; slots at or beyond the cell's count are ignored. `w_in_count`: used slots are the leading ones; in every phase each grid row has a cell with exactly 64. `w_out_slot`: positions p = d * 48 + f of a block in its cell's 12 x 48 grid of blocks; distinct within a cell; slots at or beyond the cell's count are ignored. `w_out_count`: used slots are the leading ones; in every phase each grid row has a cell with exactly 64.
All inputs are finite; a program needn't handle non-finite values.
Results may differ from the reference program's by a relative error of at most 0.012.
Values may be sent and summed in bfloat16 or wider, within the bound.
A program may use at most 128 MiB of HBM per device.

```python
import jax
import jax.numpy as jnp
from jax import lax

D = 6144
FF = 24576
BLK = 128
MICRO = 2
SECTIONS = 2
GRID_ROWS = 4
GRID_COLS = 4
MTOK = 512
DBL = 12
FBL = 48
CELL_BLOCKS = 576
NZ_MAX = 64


def cell_counts(key):
    key_base, key_heavy = jax.random.split(key)
    baseline = jax.random.randint(key_base, (SECTIONS, GRID_ROWS, GRID_COLS), NZ_MAX // 4, NZ_MAX // 2 + 1)
    heavy_col = jax.random.randint(key_heavy, (SECTIONS, GRID_ROWS, 1), 0, GRID_COLS)
    columns = jnp.arange(GRID_COLS, dtype=jnp.int32)[None, None, :]
    return jnp.where(columns == heavy_col, NZ_MAX, baseline).astype(jnp.int32)


def cell_slots(key):
    cell_keys = jax.random.split(key, SECTIONS * GRID_ROWS * GRID_COLS)
    chosen = jax.vmap(lambda single: jax.random.permutation(single, CELL_BLOCKS)[:NZ_MAX])(cell_keys)
    return chosen.reshape(SECTIONS, GRID_ROWS, GRID_COLS, NZ_MAX).astype(jnp.int32)


def draw_w_in_slot(key, part):
    return cell_slots(jax.random.fold_in(key, 21))


def draw_w_in_count(key, part):
    return cell_counts(jax.random.fold_in(key, 11))


def draw_w_out_slot(key, part):
    return cell_slots(jax.random.fold_in(key, 22))


def draw_w_out_count(key, part):
    return cell_counts(jax.random.fold_in(key, 12))


def shard_levels(own_key, extent, cuts, smallest, top_value):
    level, own = 1.0, jax.random.fold_in(own_key, 6)
    for position, parts in cuts:
        heights = jnp.exp(jax.random.uniform(jax.random.fold_in(own, position), (parts,), jnp.float32, smallest / len(cuts), top_value / len(cuts)))
        level = level * jnp.repeat(heights, extent[position] // parts).reshape([-1 if axis == position else 1 for axis in range(len(extent))])
    return level


def gaussian(key, shape, width, limit, pieces=(), kind=jnp.bfloat16):
    values = jax.random.normal(key, shape, jnp.float32) * width
    if len(pieces) > 0:
        values = shard_levels(key, shape, pieces, -0.22, 0.18) * values
    return jnp.clip(values, min=-limit, max=limit).astype(kind)


def setup_inputs(seed: int = 0) -> dict:
    seeds = jax.random.split(jax.random.key(seed), 9)
    inputs = gaussian(seeds[0], (MICRO, MTOK, D), 1.0, 6.0, ((1, 4),))
    norm_gain = jnp.clip(1.0 + 0.18 * jax.random.normal(seeds[1], (SECTIONS, D), jnp.float32), 0.1, 1.9)
    w_in = gaussian(seeds[2], (SECTIONS, GRID_ROWS, GRID_COLS, NZ_MAX, BLK, BLK), (D // 20) ** -0.5, 0.3125, ((0, 2), (1, 4), (2, 4)))
    w_in_slot = draw_w_in_slot(jax.random.fold_in(seeds[8], 71), 0)
    w_in_count = draw_w_in_count(jax.random.fold_in(seeds[8], 71), 0)
    w_out = gaussian(seeds[5], (SECTIONS, GRID_ROWS, GRID_COLS, NZ_MAX, BLK, BLK), (FF // 20) ** -0.5, 0.15625, ((0, 2), (1, 4), (2, 4)))
    w_out_slot = draw_w_out_slot(jax.random.fold_in(seeds[8], 71), 0)
    w_out_count = draw_w_out_count(jax.random.fold_in(seeds[8], 71), 0)
    return {"inputs": inputs, "norm_gain": norm_gain, "w_in": w_in, "w_in_slot": w_in_slot, "w_in_count": w_in_count, "w_out": w_out, "w_out_slot": w_out_slot, "w_out_count": w_out_count}


EPSILON = 1e-05

def feed_forward(x_rows, gain_row, in_blocks, in_slots, in_counts, out_blocks, out_slots, out_counts):
    as_float = x_rows.astype(jnp.float32)
    scaled = as_float * lax.rsqrt(lax.optimization_barrier(jnp.mean(as_float * as_float, axis=1, keepdims=True)) + EPSILON) * gain_row[None, :]
    normed = scaled.astype(jnp.bfloat16)
    token_rows = x_rows.shape[0]
    model_split = normed.reshape(token_rows, D // BLK, BLK)
    slot_range = jnp.arange(NZ_MAX, dtype=jnp.int32)
    col_range = jnp.arange(GRID_COLS, dtype=jnp.int32)
    row_range = jnp.arange(GRID_ROWS, dtype=jnp.int32)

    def hidden_step(running, row_idx):
        slot_ids = in_slots[row_idx].astype(jnp.int32)
        usable = (slot_range[None, :] < in_counts[row_idx][:, None]).astype(jnp.float32)
        model_block = (row_idx * DBL + slot_ids // FBL).astype(jnp.int32)
        hidden_block = (col_range[:, None] * FBL + slot_ids % FBL).astype(jnp.int32)
        chosen = jnp.take(model_split, model_block.reshape(-1), axis=1).astype(jnp.float32)
        weights = in_blocks[row_idx].reshape(-1, BLK, BLK).astype(jnp.float32)
        products = jnp.einsum('mek,ekf->emf', chosen, weights) * usable.reshape(-1, 1, 1)
        return (running + jax.ops.segment_sum(products, hidden_block.reshape(-1), num_segments=FF // BLK), None)
    start_hidden = jnp.zeros((FF // BLK, token_rows, BLK), jnp.float32)
    before, unused = lax.scan(hidden_step, start_hidden, row_range)
    before = jnp.transpose(before, (1, 0, 2)).reshape(token_rows, FF)
    hidden = jax.nn.gelu(before).astype(jnp.bfloat16)
    hidden_split = hidden.reshape(token_rows, FF // BLK, BLK)

    def output_step(running, col_idx):
        slot_ids = out_slots[:, col_idx].astype(jnp.int32)
        usable = (slot_range[None, :] < out_counts[:, col_idx][:, None]).astype(jnp.float32)
        hidden_block = (col_idx * FBL + slot_ids % FBL).astype(jnp.int32)
        model_block = (row_range[:, None] * DBL + slot_ids // FBL).astype(jnp.int32)
        chosen = jnp.take(hidden_split, hidden_block.reshape(-1), axis=1).astype(jnp.float32)
        weights = out_blocks[:, col_idx].reshape(-1, BLK, BLK).astype(jnp.float32)
        products = jnp.einsum('mek,ekf->emf', chosen, weights) * usable.reshape(-1, 1, 1)
        part = jax.ops.segment_sum(products, model_block.reshape(-1), num_segments=D // BLK)
        part = lax.optimization_barrier(part.astype(jnp.bfloat16)).astype(jnp.float32)
        return (running + part, None)
    start_output = jnp.zeros((D // BLK, token_rows, BLK), jnp.float32)
    summed, unused = lax.scan(output_step, start_output, col_range)
    return jnp.transpose(summed, (1, 0, 2)).reshape(token_rows, D)

def reference(inputs, norm_gain, w_in, w_in_slot, w_in_count, w_out, w_out_slot, w_out_count):
    per_phase = [[] for phase_idx in range(SECTIONS)]
    for micro_idx in range(MICRO):
        current = inputs[micro_idx]
        for phase_idx in range(SECTIONS):
            branch = feed_forward(current, norm_gain[phase_idx], w_in[phase_idx], w_in_slot[phase_idx], w_in_count[phase_idx], w_out[phase_idx], w_out_slot[phase_idx], w_out_count[phase_idx])
            current = (current.astype(jnp.float32) + branch).astype(jnp.bfloat16)
            per_phase[phase_idx].append(current)
    return jnp.stack([jnp.stack(outputs_of) for outputs_of in per_phase])
```

```python
import functools

import jax
import jax.numpy as jnp
from jax import lax
from jax.experimental import pallas as pl
from jax.experimental.pallas import tpu as pltpu
from jax.sharding import PartitionSpec as P

FF = 24576


EPSILON = 1e-05
UNROLL = 4


def add_blocks(acc, source, weights, slots, counts, offset, d_blocks, f_blocks, into_hidden):
    cells, slot_count = weights.shape[0], weights.shape[1]
    step = UNROLL if slot_count % UNROLL == 0 else 1

    def cell_body(cell, carry):
        count = counts[offset + cell]

        def group(g, inner):
            products = []
            for j in range(step):
                n = g * step + j
                usable = n < count
                p = jnp.where(usable, slots[(offset + cell) * slot_count + n], 0)
                d = cell * d_blocks + lax.div(p, f_blocks)
                f = lax.rem(p, f_blocks)
                src, dst = (d, f) if into_hidden else (f, d)
                w = weights[cell, n]
                w = jnp.where(usable, w, jnp.zeros_like(w))
                products.append(
                    (dst, jnp.dot(source[src], w, preferred_element_type=jnp.float32))
                )
            for dst, value in products:
                acc[dst] += value
            return inner

        lax.fori_loop(0, lax.div(count + step - 1, step), group, 0)
        return carry

    lax.fori_loop(0, cells, cell_body, 0)


def ffn_kernel(d_blocks, f_blocks, slots, counts, x, gain, w_in, w_out, out, normed, hidden, acc):
    cells = w_in.shape[0]
    all_d = cells * d_blocks
    tokens = x.shape[0]
    blk = w_in.shape[-1]
    total = jnp.zeros((tokens, 1), jnp.float32)
    for d in range(all_d):
        part = x[:, d * blk : (d + 1) * blk].astype(jnp.float32)
        total = total + jnp.sum(part * part, axis=1, keepdims=True)
    scale = lax.rsqrt(total / (all_d * blk) + EPSILON)
    for d in range(all_d):
        cols = slice(d * blk, (d + 1) * blk)
        normed[d] = (x[:, cols].astype(jnp.float32) * scale * gain[:, cols]).astype(jnp.bfloat16)

    def clear(i, carry):
        acc[i] = jnp.zeros_like(acc[i])
        return carry

    lax.fori_loop(0, f_blocks, clear, 0)
    add_blocks(acc, normed, w_in, slots, counts, 0, d_blocks, f_blocks, True)

    def activate(i, carry):
        hidden[i] = jax.nn.gelu(acc[i]).astype(jnp.bfloat16)
        return carry

    lax.fori_loop(0, f_blocks, activate, 0)
    lax.fori_loop(0, all_d, clear, 0)
    add_blocks(acc, hidden, w_out, slots, counts, cells, d_blocks, f_blocks, False)
    for d in range(all_d):
        out[:, d * blk : (d + 1) * blk] = acc[d].astype(jnp.bfloat16)


def ffn(x, gain, w_in, w_out, slots, counts, d_blocks, f_blocks):
    tokens, width = x.shape
    blk = w_in.shape[-1]
    vmem = pl.BlockSpec(memory_space=pltpu.VMEM)
    smem = pl.BlockSpec(memory_space=pltpu.SMEM)
    all_d = width // blk
    return pl.pallas_call(
        functools.partial(ffn_kernel, d_blocks, f_blocks),
        out_shape=jax.ShapeDtypeStruct((tokens, width), jnp.bfloat16),
        in_specs=[smem, smem, vmem, vmem, vmem, vmem],
        out_specs=vmem,
        scratch_shapes=[
            pltpu.VMEM((all_d, tokens, blk), jnp.bfloat16),
            pltpu.VMEM((f_blocks, tokens, blk), jnp.bfloat16),
            pltpu.VMEM((max(all_d, f_blocks), tokens, blk), jnp.float32),
        ],
        compiler_params=pltpu.CompilerParams(vmem_limit_bytes=52 * 2**20),
    )(slots, counts, x, gain, w_in, w_out)


def shards(inputs, norm_gain, w_in, w_in_slot, w_in_count, w_out, w_out_slot, w_out_count):
    phase_idx = lax.axis_index("section")
    col_idx = lax.axis_index("col")
    col_total = lax.axis_size("col")
    row_total = lax.axis_size("row")
    micro_count, token_rows, model_width = inputs.shape
    shard_width = model_width // col_total
    blk = w_in.shape[-1]
    d_blocks = model_width // blk // row_total
    f_blocks = FF // blk // col_total
    slot_count = w_in.shape[3]
    meta = jnp.concatenate(
        [w_in_slot.reshape(-1), w_out_slot.reshape(-1), w_in_count.reshape(-1), w_out_count.reshape(-1)]
    )
    meta = lax.all_gather(meta, "row", axis=0)
    slots = jnp.concatenate(
        [meta[:, :slot_count].reshape(-1), meta[:, slot_count : 2 * slot_count].reshape(-1)]
    )
    counts = jnp.concatenate([meta[:, 2 * slot_count], meta[:, 2 * slot_count + 1]])
    all_in = lax.all_gather(w_in[0, 0, 0], "row", axis=0)
    all_out = lax.all_gather(w_out[0, 0, 0], "row", axis=0)
    tokens = micro_count * token_rows

    current_full = inputs.reshape(tokens, model_width)
    current = lax.dynamic_slice_in_dim(current_full, col_idx * shard_width, shard_width, 1)
    results = []
    phases = lax.axis_size("section")
    for phase in range(phases):
        part = ffn(current_full, norm_gain, all_in, all_out, slots, counts, d_blocks, f_blocks)
        branch = lax.psum_scatter(part, "col", scatter_dimension=1, tiled=True)
        result = (current.astype(jnp.float32) + branch.astype(jnp.float32)).astype(jnp.bfloat16)
        results.append(result)
        if phase + 1 < phases:
            current = lax.ppermute(result, "section", [(i, i + 1) for i in range(phases - 1)])
            current_full = lax.all_gather(current, "col", axis=1, tiled=True)
    out = results[0]
    for phase in range(1, phases):
        out = jnp.where(phase_idx == phase, results[phase], out)
    return out.reshape(1, micro_count, token_rows, shard_width)


def solution(mesh):
    placed = (
        P(None, "row", None),
        P("section", None),
        P("section", "row", "col", None, None, None),
        P("section", "row", "col", None),
        P("section", "row", "col"),
        P("section", "row", "col", None, None, None),
        P("section", "row", "col", None),
        P("section", "row", "col"),
    )
    return jax.shard_map(
        shards,
        mesh=mesh,
        in_specs=placed,
        out_specs=P("section", None, "row", "col"),
        check_vma=False,
    )
```

```python
import functools

import jax
import jax.numpy as jnp
from jax import lax
from jax.experimental import pallas as pl
from jax.experimental.pallas import tpu as pltpu
from jax.sharding import PartitionSpec as P

FF = 24576


EPSILON = 1e-05
UNROLL = 4


def add_blocks(acc, source, weights, slots, counts, offset, d_blocks, f_blocks, into_hidden):
    cells, slot_count = weights.shape[0], weights.shape[1]
    step = UNROLL if slot_count % UNROLL == 0 else 1

    def cell_body(cell, carry):
        count = counts[offset + cell]

        def group(g, inner):
            products = []
            for j in range(step):
                n = g * step + j
                usable = n < count
                p = jnp.where(usable, slots[(offset + cell) * slot_count + n], 0)
                d = cell * d_blocks + lax.div(p, f_blocks)
                f = lax.rem(p, f_blocks)
                src, dst = (d, f) if into_hidden else (f, d)
                w = weights[cell, n]
                w = jnp.where(usable, w, jnp.zeros_like(w))
                products.append(
                    (dst, jnp.dot(source[src], w, preferred_element_type=jnp.float32))
                )
            for dst, value in products:
                acc[dst] += value
            return inner

        lax.fori_loop(0, lax.div(count + step - 1, step), group, 0)
        return carry

    lax.fori_loop(0, cells, cell_body, 0)


def clear_blocks(acc, count):
    def body(i, carry):
        acc[i] = jnp.zeros_like(acc[i])
        return carry

    lax.fori_loop(0, count, body, 0)


def hidden_kernel(d_blocks, f_blocks, active, slots, counts, x, gain, w_in, hidden, normed, acc):
    @pl.when(active[0] == 1)
    def _():
        cells = w_in.shape[0]
        all_d = cells * d_blocks
        blk = w_in.shape[-1]
        total = jnp.zeros((x.shape[0], 1), jnp.float32)
        for d in range(all_d):
            part = x[:, d * blk : (d + 1) * blk].astype(jnp.float32)
            total = total + jnp.sum(part * part, axis=1, keepdims=True)
        scale = lax.rsqrt(total / (all_d * blk) + EPSILON)
        for d in range(all_d):
            cols = slice(d * blk, (d + 1) * blk)
            normed[d] = (x[:, cols].astype(jnp.float32) * scale * gain[:, cols]).astype(jnp.bfloat16)
        clear_blocks(acc, f_blocks)
        add_blocks(acc, normed, w_in, slots, counts, 0, d_blocks, f_blocks, True)

        def activate(i, carry):
            hidden[i] = jax.nn.gelu(acc[i]).astype(jnp.bfloat16)
            return carry

        lax.fori_loop(0, f_blocks, activate, 0)


def part_kernel(d_blocks, f_blocks, active, slots, counts, hidden, w_out, out, acc):
    @pl.when(active[0] == 1)
    def _():
        cells = w_out.shape[0]
        all_d = cells * d_blocks
        blk = w_out.shape[-1]
        clear_blocks(acc, all_d)
        add_blocks(acc, hidden, w_out, slots, counts, cells, d_blocks, f_blocks, False)
        for d in range(all_d):
            out[:, d * blk : (d + 1) * blk] = acc[d].astype(jnp.bfloat16)


VMEM = pl.BlockSpec(memory_space=pltpu.VMEM)
SMEM = pl.BlockSpec(memory_space=pltpu.SMEM)


def cost(tokens, weights):
    return pl.CostEstimate(
        flops=2 * tokens * weights.size, bytes_accessed=2 * weights.size, transcendentals=0
    )


def hidden_call(active, slots, counts, x, gain, w_in, d_blocks, f_blocks):
    tokens, width = x.shape
    blk = w_in.shape[-1]
    return pl.pallas_call(
        functools.partial(hidden_kernel, d_blocks, f_blocks),
        out_shape=jax.ShapeDtypeStruct((f_blocks, tokens, blk), jnp.bfloat16),
        in_specs=[SMEM, SMEM, SMEM, VMEM, VMEM, VMEM],
        out_specs=VMEM,
        scratch_shapes=[
            pltpu.VMEM((width // blk, tokens, blk), jnp.bfloat16),
            pltpu.VMEM((f_blocks, tokens, blk), jnp.float32),
        ],
        compiler_params=pltpu.CompilerParams(vmem_limit_bytes=40 * 2**20),
        cost_estimate=cost(tokens, w_in),
    )(active, slots, counts, x, gain, w_in)


def part_call(active, slots, counts, hidden, w_out, d_blocks, f_blocks):
    tokens, blk = hidden.shape[1:]
    all_d = w_out.shape[0] * d_blocks
    return pl.pallas_call(
        functools.partial(part_kernel, d_blocks, f_blocks),
        out_shape=jax.ShapeDtypeStruct((tokens, all_d * blk), jnp.bfloat16),
        in_specs=[SMEM, SMEM, SMEM, VMEM, VMEM],
        out_specs=VMEM,
        scratch_shapes=[pltpu.VMEM((all_d, tokens, blk), jnp.float32)],
        compiler_params=pltpu.CompilerParams(vmem_limit_bytes=40 * 2**20),
        cost_estimate=cost(tokens, w_out),
    )(active, slots, counts, hidden, w_out)


def combine_kernel(phase, passes_on, part, current, *refs):
    if passes_on:
        result, full, landed, send_sem, recv_sem, push_sem, full_sem = refs
    else:
        result, landed, send_sem, recv_sem = refs
    cols = lax.axis_size("col")
    width = current.shape[1]
    mine = lax.axis_index("section")
    col = lax.axis_index("col")
    barrier = pltpu.get_barrier_semaphore()

    def device(section, other):
        return {"section": section, "col": other}

    def columns(c):
        return pl.ds(pl.multiple_of(c * width, width), width)

    def share(k):
        other = lax.rem(col + k, cols)
        return pltpu.make_async_remote_copy(
            src_ref=part.at[:, columns(other)],
            dst_ref=landed.at[k - 1],
            send_sem=send_sem.at[k - 1],
            recv_sem=recv_sem.at[k - 1],
            device_id=device(phase, other),
            device_id_type=pl.DeviceIdType.MESH,
        )

    def push(k):
        other = lax.rem(col + k, cols)
        return pltpu.make_async_remote_copy(
            src_ref=result,
            dst_ref=full.at[:, columns(col)],
            send_sem=push_sem.at[k],
            recv_sem=full_sem.at[k],
            device_id=device(phase + 1, other),
            device_id_type=pl.DeviceIdType.MESH,
        )

    @pl.when(mine == phase)
    def _():
        for k in range(1, cols):
            other = lax.rem(col + k, cols)
            pl.semaphore_signal(
                barrier, inc=1, device_id=device(phase, other), device_id_type=pl.DeviceIdType.MESH
            )
        if passes_on:
            for k in range(cols):
                other = lax.rem(col + k, cols)
                pl.semaphore_signal(
                    barrier, inc=1, device_id=device(phase + 1, other), device_id_type=pl.DeviceIdType.MESH
                )
        pl.semaphore_wait(barrier, 2 * cols - 1 if passes_on else cols - 1)
        shares = [share(k) for k in range(1, cols)]
        for copy in shares:
            copy.start()
        for copy in shares:
            copy.wait()
        total = part[:, columns(col)].astype(jnp.float32)
        for k in range(1, cols):
            total = total + landed[k - 1].astype(jnp.float32)
        result[...] = (current[...].astype(jnp.float32) + total).astype(jnp.bfloat16)
        if passes_on:
            pushes = [push(k) for k in range(cols)]
            for copy in pushes:
                copy.start()
            for copy in pushes:
                copy.wait_send()

    if passes_on:
        @pl.when(mine == phase + 1)
        def _():
            for k in range(cols):
                other = lax.rem(col + k, cols)
                pl.semaphore_signal(
                    barrier, inc=1, device_id=device(phase, other), device_id_type=pl.DeviceIdType.MESH
                )
            pl.semaphore_wait(barrier, cols)
            for k in range(cols):
                source = lax.rem(col + cols - k, cols)
                pltpu.make_async_remote_copy(
                    src_ref=result,
                    dst_ref=full.at[:, columns(source)],
                    send_sem=push_sem.at[k],
                    recv_sem=full_sem.at[k],
                    device_id=device(phase, source),
                    device_id_type=pl.DeviceIdType.MESH,
                ).wait_recv()


def combine(phase, passes_on, part, current):
    tokens, width = current.shape
    cols = part.shape[1] // width
    shapes = [jax.ShapeDtypeStruct(current.shape, jnp.bfloat16)]
    sems = [pltpu.SemaphoreType.DMA((cols,))] * 2
    if passes_on:
        shapes.append(jax.ShapeDtypeStruct(part.shape, jnp.bfloat16))
        sems = sems * 2
    return pl.pallas_call(
        functools.partial(combine_kernel, phase, passes_on),
        out_shape=shapes,
        in_specs=[VMEM, VMEM],
        out_specs=[VMEM] * len(shapes),
        scratch_shapes=[pltpu.VMEM((cols, tokens, width), jnp.bfloat16)] + sems,
        compiler_params=pltpu.CompilerParams(
            collective_id=phase, has_side_effects=True, vmem_limit_bytes=32 * 2**20
        ),
        cost_estimate=pl.CostEstimate(
            flops=part.size, bytes_accessed=16 * part.size, transcendentals=0
        ),
    )(part, current)


def shards(inputs, norm_gain, w_in, w_in_slot, w_in_count, w_out, w_out_slot, w_out_count):
    phase_idx = lax.axis_index("section")
    col_idx = lax.axis_index("col")
    col_total = lax.axis_size("col")
    row_total = lax.axis_size("row")
    micro_count, token_rows, model_width = inputs.shape
    shard_width = model_width // col_total
    blk = w_in.shape[-1]
    d_blocks = model_width // blk // row_total
    f_blocks = FF // blk // col_total
    slot_count = w_in.shape[3]
    own_in, own_out = w_in[0, 0, 0], w_out[0, 0, 0]
    sibling_out = lax.ppermute(own_out, "section", [(0, 1), (1, 0)])
    carried = [
        lax.all_gather(jnp.where(phase_idx == 0, own_in, sibling_out), "row", axis=0)
    ]
    meta = jnp.concatenate(
        [w_in_slot.reshape(-1), w_out_slot.reshape(-1), w_in_count.reshape(-1), w_out_count.reshape(-1)]
    )
    meta = lax.all_gather(meta, "row", axis=0)
    second, first, meta = lax.optimization_barrier(
        (jnp.where(phase_idx == 1, own_in, sibling_out), carried[0], meta)
    )
    carried = [first, lax.all_gather(second, "row", axis=0)]
    slots = jnp.concatenate(
        [meta[:, :slot_count].reshape(-1), meta[:, slot_count : 2 * slot_count].reshape(-1)]
    )
    counts = jnp.concatenate([meta[:, 2 * slot_count], meta[:, 2 * slot_count + 1]])
    tokens = micro_count * token_rows

    full = inputs.reshape(tokens, model_width)
    current = lax.dynamic_slice_in_dim(full, col_idx * shard_width, shard_width, 1)
    results = []
    for phase in range(2):
        active = (phase_idx == phase).astype(jnp.int32).reshape(1)
        out_weights = lax.ppermute(carried[phase], "section", [(1 - phase, phase)])
        hidden = hidden_call(active, slots, counts, full, norm_gain, carried[phase], d_blocks, f_blocks)
        part = part_call(active, slots, counts, hidden, out_weights, d_blocks, f_blocks)
        if phase == 0:
            result, full = combine(0, True, part, current)
            full, carried[1] = lax.optimization_barrier((full, carried[1]))
            current = lax.dynamic_slice_in_dim(full, col_idx * shard_width, shard_width, 1)
        else:
            [result] = combine(1, False, part, current)
        results.append(result)
    out = jnp.where(phase_idx == 0, results[0], results[1])
    return out.reshape(1, micro_count, token_rows, shard_width)


def solution(mesh):
    placed = (
        P(None, "row", None),
        P("section", None),
        P("section", "row", "col", None, None, None),
        P("section", "row", "col", None),
        P("section", "row", "col"),
        P("section", "row", "col", None, None, None),
        P("section", "row", "col", None),
        P("section", "row", "col"),
    )
    return jax.shard_map(
        shards,
        mesh=mesh,
        in_specs=placed,
        out_specs=P("section", None, "row", "col"),
        check_vma=False,
    )
```

```python
import functools
import math

import jax
import jax.numpy as jnp
from jax import lax
from jax.experimental import pallas as pl
from jax.experimental.pallas import tpu as pltpu
from jax.sharding import PartitionSpec as P

FF = 24576


EPSILON = 1e-05
UNROLL = 8


def add_blocks(acc, source, weights, slots, counts, base, offset, d_blocks, f_blocks, into_hidden):
    cells, held = weights.shape[0], weights.shape[1]
    slot_count = slots.shape[0] // (2 * cells)
    step = math.gcd(UNROLL, held)

    def cell_body(cell, carry):
        count = jnp.clip(counts[offset + cell] - base, 0, held)

        def group(g, inner):
            products = []
            for j in range(step):
                n = g * step + j
                usable = n < count
                p = jnp.where(usable, slots[(offset + cell) * slot_count + base + n], 0)
                d = cell * d_blocks + lax.div(p, f_blocks)
                f = lax.rem(p, f_blocks)
                src, dst = (d, f) if into_hidden else (f, d)
                w = weights[cell, n]
                w = jnp.where(usable, w, jnp.zeros_like(w))
                products.append(
                    (dst, jnp.dot(source[src], w, preferred_element_type=jnp.float32))
                )
            for dst, value in products:
                acc[dst] += value
            return inner

        lax.fori_loop(0, lax.div(count + step - 1, step), group, 0)
        return carry

    lax.fori_loop(0, cells, cell_body, 0)


def clear_blocks(acc, count):
    def body(i, carry):
        acc[i] = jnp.zeros_like(acc[i])
        return carry

    lax.fori_loop(0, count, body, 0)


def add_all(acc, source, pieces, slots, counts, offset, d_blocks, f_blocks, into_hidden):
    base = 0
    for piece in pieces:
        add_blocks(acc, source, piece, slots, counts, base, offset, d_blocks, f_blocks, into_hidden)
        base += piece.shape[1]


def hidden_kernel(d_blocks, f_blocks, active, slots, counts, x, gain, *refs):
    *pieces, hidden, normed, acc = refs
    w_in = pieces[0]

    @pl.when(active[0] == 1)
    def _():
        cells = w_in.shape[0]
        all_d = cells * d_blocks
        blk = w_in.shape[-1]
        total = jnp.zeros((x.shape[0], 1), jnp.float32)
        for d in range(all_d):
            part = x[:, d * blk : (d + 1) * blk].astype(jnp.float32)
            total = total + jnp.sum(part * part, axis=1, keepdims=True)
        scale = lax.rsqrt(total / (all_d * blk) + EPSILON)
        for d in range(all_d):
            cols = slice(d * blk, (d + 1) * blk)
            normed[d] = (x[:, cols].astype(jnp.float32) * scale * gain[:, cols]).astype(jnp.bfloat16)
        clear_blocks(acc, f_blocks)
        add_all(acc, normed, pieces, slots, counts, 0, d_blocks, f_blocks, True)

        def activate(i, carry):
            hidden[i] = jax.nn.gelu(acc[i]).astype(jnp.bfloat16)
            return carry

        lax.fori_loop(0, f_blocks, activate, 0)


def part_kernel(d_blocks, f_blocks, active, slots, counts, hidden, *refs):
    *pieces, out, acc = refs
    w_out = pieces[0]

    @pl.when(active[0] == 1)
    def _():
        cells = w_out.shape[0]
        all_d = cells * d_blocks
        blk = w_out.shape[-1]
        clear_blocks(acc, all_d)
        add_all(acc, hidden, pieces, slots, counts, cells, d_blocks, f_blocks, False)
        for d in range(all_d):
            out[:, d * blk : (d + 1) * blk] = acc[d].astype(jnp.bfloat16)


VMEM = pl.BlockSpec(memory_space=pltpu.VMEM)
SMEM = pl.BlockSpec(memory_space=pltpu.SMEM)


def cost(tokens, pieces):
    size = sum(piece.size for piece in pieces)
    return pl.CostEstimate(
        flops=2 * tokens * size, bytes_accessed=2 * size, transcendentals=0
    )


def hidden_call(active, slots, counts, x, gain, pieces, d_blocks, f_blocks):
    tokens, width = x.shape
    blk = pieces[0].shape[-1]
    return pl.pallas_call(
        functools.partial(hidden_kernel, d_blocks, f_blocks),
        out_shape=jax.ShapeDtypeStruct((f_blocks, tokens, blk), jnp.bfloat16),
        in_specs=[SMEM, SMEM, SMEM, VMEM, VMEM] + [VMEM] * len(pieces),
        out_specs=VMEM,
        scratch_shapes=[
            pltpu.VMEM((width // blk, tokens, blk), jnp.bfloat16),
            pltpu.VMEM((f_blocks, tokens, blk), jnp.float32),
        ],
        compiler_params=pltpu.CompilerParams(vmem_limit_bytes=40 * 2**20),
        cost_estimate=cost(tokens, pieces),
    )(active, slots, counts, x, gain, *pieces)


def part_call(active, slots, counts, hidden, pieces, d_blocks, f_blocks):
    tokens, blk = hidden.shape[1:]
    all_d = pieces[0].shape[0] * d_blocks
    return pl.pallas_call(
        functools.partial(part_kernel, d_blocks, f_blocks),
        out_shape=jax.ShapeDtypeStruct((tokens, all_d * blk), jnp.bfloat16),
        in_specs=[SMEM, SMEM, SMEM, VMEM] + [VMEM] * len(pieces),
        out_specs=VMEM,
        scratch_shapes=[pltpu.VMEM((all_d, tokens, blk), jnp.float32)],
        compiler_params=pltpu.CompilerParams(vmem_limit_bytes=40 * 2**20),
        cost_estimate=cost(tokens, pieces),
    )(active, slots, counts, hidden, *pieces)


def combine_kernel(phase, passes_on, part, current, *refs):
    if passes_on:
        result, full, landed, send_sem, recv_sem, push_sem, full_sem = refs
    else:
        result, landed, send_sem, recv_sem = refs
    cols = lax.axis_size("col")
    width = current.shape[1]
    mine = lax.axis_index("section")
    col = lax.axis_index("col")
    barrier = pltpu.get_barrier_semaphore()

    def device(section, other):
        return {"section": section, "col": other}

    def columns(c):
        return pl.ds(pl.multiple_of(c * width, width), width)

    def share(k):
        other = lax.rem(col + k, cols)
        return pltpu.make_async_remote_copy(
            src_ref=part.at[:, columns(other)],
            dst_ref=landed.at[k - 1],
            send_sem=send_sem.at[k - 1],
            recv_sem=recv_sem.at[k - 1],
            device_id=device(phase, other),
            device_id_type=pl.DeviceIdType.MESH,
        )

    def push(k):
        other = lax.rem(col + k, cols)
        return pltpu.make_async_remote_copy(
            src_ref=result,
            dst_ref=full.at[:, columns(col)],
            send_sem=push_sem.at[k],
            recv_sem=full_sem.at[k],
            device_id=device(phase + 1, other),
            device_id_type=pl.DeviceIdType.MESH,
        )

    @pl.when(mine == phase)
    def _():
        for k in range(1, cols):
            other = lax.rem(col + k, cols)
            pl.semaphore_signal(
                barrier, inc=1, device_id=device(phase, other), device_id_type=pl.DeviceIdType.MESH
            )
        if passes_on:
            for k in range(cols):
                other = lax.rem(col + k, cols)
                pl.semaphore_signal(
                    barrier, inc=1, device_id=device(phase + 1, other), device_id_type=pl.DeviceIdType.MESH
                )
        pl.semaphore_wait(barrier, 2 * cols - 1 if passes_on else cols - 1)
        shares = [share(k) for k in range(1, cols)]
        for copy in shares:
            copy.start()
        for copy in shares:
            copy.wait()
        total = part[:, columns(col)].astype(jnp.float32)
        for k in range(1, cols):
            total = total + landed[k - 1].astype(jnp.float32)
        result[...] = (current[...].astype(jnp.float32) + total).astype(jnp.bfloat16)
        if passes_on:
            pushes = [push(k) for k in range(cols)]
            for copy in pushes:
                copy.start()
            for copy in pushes:
                copy.wait_send()

    if passes_on:
        @pl.when(mine == phase + 1)
        def _():
            for k in range(cols):
                other = lax.rem(col + k, cols)
                pl.semaphore_signal(
                    barrier, inc=1, device_id=device(phase, other), device_id_type=pl.DeviceIdType.MESH
                )
            pl.semaphore_wait(barrier, cols)
            for k in range(cols):
                source = lax.rem(col + cols - k, cols)
                pltpu.make_async_remote_copy(
                    src_ref=result,
                    dst_ref=full.at[:, columns(source)],
                    send_sem=push_sem.at[k],
                    recv_sem=full_sem.at[k],
                    device_id=device(phase, source),
                    device_id_type=pl.DeviceIdType.MESH,
                ).wait_recv()


def combine(phase, passes_on, part, current):
    tokens, width = current.shape
    cols = part.shape[1] // width
    shapes = [jax.ShapeDtypeStruct(current.shape, jnp.bfloat16)]
    sems = [pltpu.SemaphoreType.DMA((cols,))] * 2
    if passes_on:
        shapes.append(jax.ShapeDtypeStruct(part.shape, jnp.bfloat16))
        sems = sems * 2
    return pl.pallas_call(
        functools.partial(combine_kernel, phase, passes_on),
        out_shape=shapes,
        in_specs=[VMEM, VMEM],
        out_specs=[VMEM] * len(shapes),
        scratch_shapes=[pltpu.VMEM((cols, tokens, width), jnp.bfloat16)] + sems,
        compiler_params=pltpu.CompilerParams(
            collective_id=phase, has_side_effects=True, vmem_limit_bytes=32 * 2**20
        ),
        cost_estimate=pl.CostEstimate(
            flops=part.size, bytes_accessed=16 * part.size, transcendentals=0
        ),
    )(part, current)


def shards(inputs, norm_gain, w_in, w_in_slot, w_in_count, w_out, w_out_slot, w_out_count):
    phase_idx = lax.axis_index("section")
    col_idx = lax.axis_index("col")
    col_total = lax.axis_size("col")
    row_total = lax.axis_size("row")
    micro_count, token_rows, model_width = inputs.shape
    shard_width = model_width // col_total
    blk = w_in.shape[-1]
    d_blocks = model_width // blk // row_total
    f_blocks = FF // blk // col_total
    slot_count = w_in.shape[3]
    own_in, own_out = w_in[0, 0, 0], w_out[0, 0, 0]
    half = slot_count // 2
    first_out = lax.ppermute(own_out, "section", [(0, 1)])
    upper = lax.ppermute(jnp.concatenate([own_in[half:], own_out[half:]]), "section", [(1, 0)])
    first = lax.all_gather(jnp.where(phase_idx == 0, own_in, first_out), "row", axis=0)
    meta = jnp.concatenate(
        [w_in_slot.reshape(-1), w_out_slot.reshape(-1), w_in_count.reshape(-1), w_out_count.reshape(-1)]
    )
    meta = lax.all_gather(meta, "row", axis=0)
    second, third, first, meta = lax.optimization_barrier(
        (
            jnp.where(phase_idx == 1, own_in[:half], upper[: slot_count - half]),
            jnp.where(phase_idx == 1, own_out[:half], upper[slot_count - half :]),
            first,
            meta,
        )
    )
    second = lax.all_gather(second, "row", axis=0)
    slots = jnp.concatenate(
        [meta[:, :slot_count].reshape(-1), meta[:, slot_count : 2 * slot_count].reshape(-1)]
    )
    counts = jnp.concatenate([meta[:, 2 * slot_count], meta[:, 2 * slot_count + 1]])
    tokens = micro_count * token_rows

    full = inputs.reshape(tokens, model_width)
    current = lax.dynamic_slice_in_dim(full, col_idx * shard_width, shard_width, 1)
    sizes = (d_blocks, f_blocks)
    active = (phase_idx == 0).astype(jnp.int32).reshape(1)
    out_weights = lax.ppermute(first, "section", [(1, 0)])
    hidden = hidden_call(active, slots, counts, full, norm_gain, [first], *sizes)
    part = part_call(active, slots, counts, hidden, [out_weights], *sizes)
    earlier, full = combine(0, True, part, current)

    full, second, third = lax.optimization_barrier((full, second, third))
    third = lax.all_gather(third, "row", axis=0)
    active = (phase_idx == 1).astype(jnp.int32).reshape(1)
    current = lax.dynamic_slice_in_dim(full, col_idx * shard_width, shard_width, 1)
    rest = lax.ppermute(second, "section", [(0, 1)])
    hidden = hidden_call(active, slots, counts, full, norm_gain, [second, rest], *sizes)
    hidden, third = lax.optimization_barrier((hidden, third))
    rest = lax.ppermute(third, "section", [(0, 1)])
    part = part_call(active, slots, counts, hidden, [third, rest], *sizes)
    [later] = combine(1, False, part, current)
    out = jnp.where(phase_idx == 0, earlier, later)
    return out.reshape(1, micro_count, token_rows, shard_width)


def solution(mesh):
    placed = (
        P(None, "row", None),
        P("section", None),
        P("section", "row", "col", None, None, None),
        P("section", "row", "col", None),
        P("section", "row", "col"),
        P("section", "row", "col", None, None, None),
        P("section", "row", "col", None),
        P("section", "row", "col"),
    )
    return jax.shard_map(
        shards,
        mesh=mesh,
        in_specs=placed,
        out_specs=P("section", None, "row", "col"),
        check_vma=False,
    )
```
